256 devices in a mesh: blk: 32 (over z, x), uly: 8 (over y, core).
Axes of the slice: x: 4, y: 4, z: 8, core: 2. Of those that a mesh axis runs over, the one named last changes fastest.
Arguments:
- q_raw: bfloat16 [4608, 24, 128], P('blk', 'uly'), may hold values from -120 to 120
- k_raw: bfloat16 [4608, 24, 128], P('blk', 'uly'), may hold values from -120 to 120
- values: bfloat16 [4608, 24, 128], P('blk', 'uly'), may hold values from -6 to 6
- out_grad: bfloat16 [4608, 24, 128], P('blk', 'uly'), may hold values from -16 to 16
- q_gain: float32 [2, 128], replicated, may hold values from 0.5 to 6.5
- k_gain: float32 [2, 128], replicated, may hold values from 0.5 to 6.5
Outputs:
- q_grad: bfloat16 [4608, 24, 128], P('blk', 'uly')
- k_grad: bfloat16 [4608, 24, 128], P('blk', 'uly')
- v_grad: bfloat16 [4608, 24, 128], P('blk', 'uly')
- q_gain_grad: float32 [2, 128], replicated
- k_gain_grad: float32 [2, 128], replicated
The draws below stay inside these ranges and needn't reach their ends.
All inputs are finite; a program needn't handle non-finite values.
Results may differ from the reference program's by a relative error of at most 0.009.
The reference program's roundings to bfloat16 on the way (of `probs_low`) count: a program that leaves them out, or rounds other values in their place, can miss the bound.
Values may be sent and summed in bfloat16 or wider, within the bound.
No kernel may reach another device: no remote copies, remote signals or barrier semaphores. Data moves between devices by JAX's collectives and lax.ppermute only.
A program may use at most 64 MiB of HBM per device.

```python
import math
import jax
import jax.numpy as jnp
from jax import lax

HEADS = 24
HD = 128
TXT = 512
SEQ = 4608


def scaled_normal(key, shape):
    noise_key, row_key, col_key = jax.random.split(key, 3)
    base = jnp.clip(jax.random.normal(noise_key, shape, jnp.float32), -6.0, 6.0)
    row_scale = jnp.exp(jax.random.uniform(row_key, (shape[0], shape[1], 1), jnp.float32, 0.0, math.log(10.0)))
    col_scale = jnp.exp(jax.random.uniform(col_key, (1, 1, shape[2]), jnp.float32, math.log(0.5), math.log(2.0)))
    return base * row_scale * col_scale


def raw_pair(key):
    base_key = jax.random.fold_in(key, 101)
    split_keys = jax.random.split(base_key, 2)
    shape = (SEQ, HEADS, HD)
    queries = scaled_normal(split_keys[0], shape)
    key_rows = scaled_normal(split_keys[1], shape)
    return (jnp.clip(queries, -120.0, 120.0), jnp.clip(key_rows, -120.0, 120.0))


def draw_q_raw(key, part):
    return raw_pair(key)[0].astype(jnp.bfloat16)


def draw_k_raw(key, part):
    return raw_pair(key)[1].astype(jnp.bfloat16)


def draw_out_grad(key, part):
    local_key = jax.random.fold_in(key, 202)
    position = jnp.arange(SEQ).astype(jnp.float32)
    rising = (1.0 + 2.0 * position / SEQ)[:, None, None]
    base = jnp.clip(jax.random.normal(local_key, (SEQ, HEADS, HD), jnp.float32), -5.0, 5.0) * rising
    return base.astype(jnp.bfloat16)


def gain_draw(key, salt):
    local_key = jax.random.fold_in(key, salt)
    return jnp.exp(jax.random.uniform(local_key, (2, HD), jnp.float32, math.log(0.5), math.log(2.0)))


def draw_q_gain(key, part):
    return gain_draw(key, 303)


def draw_k_gain(key, part):
    return gain_draw(key, 404)


def levels(key, shape, cuts, least, top_value):
    level = 1.0
    for dim, blocks in cuts:
        steps = jax.random.uniform(jax.random.fold_in(jax.random.fold_in(key, 6), dim), (blocks,), jnp.float32, least / len(cuts), top_value / len(cuts))
        level = level * jnp.repeat(jnp.exp(steps), shape[dim] // blocks).reshape((-1,) + (1,) * (len(shape) - 1 - dim))
    return level


def gaussian(stream_key, shape, spread, limit, cuts=(), kind=jnp.bfloat16):
    entries = jax.random.normal(stream_key, shape, jnp.float32) * spread
    if len(cuts) > 0:
        entries = levels(stream_key, shape, cuts, -0.22, 0.18) * entries
    return jnp.clip(entries, min=-limit, max=limit).astype(kind)


def setup_inputs(seed: int = 0) -> dict:
    key_list = jax.random.split(jax.random.key(seed), 7)
    q_raw = draw_q_raw(jax.random.fold_in(key_list[6], 71), 0)
    k_raw = draw_k_raw(jax.random.fold_in(key_list[6], 71), 0)
    values = gaussian(key_list[2], (SEQ, HEADS, HD), 1.0, 6.0, ((0, 32), (1, 8)))
    out_grad = draw_out_grad(jax.random.fold_in(key_list[6], 71), 0)
    q_gain = draw_q_gain(jax.random.fold_in(key_list[6], 71), 0)
    k_gain = draw_k_gain(jax.random.fold_in(key_list[6], 71), 0)
    return dict(q_raw=q_raw, k_raw=k_raw, values=values, out_grad=out_grad, q_gain=q_gain, k_gain=k_gain)


epsilon = 1e-06

def gain_rows(gain, position):
    return jnp.where((position < TXT)[:, None], gain[0][None, :], gain[1][None, :])

def normalize(raw, gains):
    widened = raw.astype(jnp.float32)
    root_mean = jnp.sqrt(lax.optimization_barrier(jnp.mean(widened * widened, axis=-1, keepdims=True)) + epsilon)
    unit = widened / root_mean
    return (unit, root_mean, (unit * gains[:, None, :]).astype(jnp.bfloat16))

def norm_back(grad_norm, unit, root_mean, gains):
    grad_unit = grad_norm * gains[:, None, :]
    return (grad_unit - unit * lax.optimization_barrier(jnp.mean(grad_unit * unit, axis=-1, keepdims=True))) / root_mean

def gain_parts(grad_norm, unit, position):
    per_row = lax.optimization_barrier(jnp.sum(grad_norm * unit, axis=1))
    text_rows = (position < TXT)[:, None]
    return jnp.stack([lax.optimization_barrier(jnp.sum(jnp.where(text_rows, per_row, 0.0), axis=0)), lax.optimization_barrier(jnp.sum(jnp.where(text_rows, 0.0, per_row), axis=0))])

def heads_first(array):
    return jnp.transpose(array, (1, 0, 2))

def reference(q_raw, k_raw, values, out_grad, q_gain, k_gain):
    position = jnp.arange(SEQ, dtype=jnp.int32)
    factor = 1.0 / math.sqrt(HD)
    q_gains = gain_rows(q_gain, position)
    k_gains = gain_rows(k_gain, position)
    q_unit, q_root, q_norm = normalize(q_raw, q_gains)
    k_unit, k_root, k_norm = normalize(k_raw, k_gains)

    def per_head(members):
        q_head, k_head, v_head, g_head = members
        head_scores = jnp.dot(q_head, k_head.T, preferred_element_type=jnp.float32) * factor
        peak = lax.optimization_barrier(jnp.max(head_scores, axis=1, keepdims=True))
        log_total = peak + jnp.log(lax.optimization_barrier(jnp.sum(jnp.exp(head_scores - peak), axis=1, keepdims=True)))
        probs = jnp.exp(head_scores - log_total)
        probs_low = probs.astype(jnp.bfloat16)
        attn = jnp.dot(probs, v_head.astype(jnp.float32), precision=lax.Precision.HIGHEST, preferred_element_type=jnp.float32)
        row_dot = lax.optimization_barrier(jnp.sum(g_head.astype(jnp.float32) * attn, axis=1, keepdims=True))
        grad_probs = jnp.dot(g_head, v_head.T, preferred_element_type=jnp.float32)
        mixed = (probs * grad_probs).astype(jnp.bfloat16)
        weighted_grad = jnp.dot(mixed, k_head, preferred_element_type=jnp.float32)
        weighted_keys = jnp.dot(probs_low, k_head, preferred_element_type=jnp.float32)
        grad_query = factor * (weighted_grad - row_dot * weighted_keys)
        grad_scores = (probs * (grad_probs - row_dot)).astype(jnp.bfloat16)
        grad_key = factor * jnp.dot(grad_scores.T, q_head, preferred_element_type=jnp.float32)
        grad_value = jnp.dot(probs_low.T, g_head, preferred_element_type=jnp.float32)
        return (grad_query, grad_key, grad_value)
    grad_query, grad_key, grad_value = lax.map(per_head, (heads_first(q_norm), heads_first(k_norm), heads_first(values), heads_first(out_grad)))
    grad_q_norm = heads_first(grad_query)
    grad_k_norm = heads_first(grad_key)
    v_grad = heads_first(grad_value).astype(jnp.bfloat16)
    q_grad = norm_back(grad_q_norm, q_unit, q_root, q_gains).astype(jnp.bfloat16)
    k_grad = norm_back(grad_k_norm, k_unit, k_root, k_gains).astype(jnp.bfloat16)
    q_gain_grad = gain_parts(grad_q_norm, q_unit, position)
    k_gain_grad = gain_parts(grad_k_norm, k_unit, position)
    return (q_grad, k_grad, v_grad, q_gain_grad, k_gain_grad)
```

```python
import functools
import math

import jax
import jax.numpy as jnp
from jax import lax
from jax.experimental import pallas as pl
from jax.experimental.pallas import tpu as pltpu
from jax.sharding import Mesh
from jax.sharding import PartitionSpec as P

TXT = 512
EPS = 1e-06
NH, HD, BR = 3, 128, 144
NQ, NX, NZ = 4, 4, 2
QR = NQ * BR
KC = NZ * BR
KR = NX * KC
FACTOR = 1.0 / math.sqrt(HD)
SCALE2 = FACTOR * math.log2(math.e)
F32, BF16 = jnp.float32, jnp.bfloat16
ALL_ROWS = ("zq", "zk", "x")


def nt_dot(a, b):
    return lax.dot_general(a, b, (((1,), (1,)), ((), ())), preferred_element_type=F32)


def nn_dot(a, b):
    return lax.dot_general(a, b, (((1,), (0,)), ((), ())), preferred_element_type=F32)


def tn_dot(a, b):
    return lax.dot_general(a, b, (((0,), (0,)), ((), ())), preferred_element_type=F32)


def text_mask(block):
    row = block * BR + lax.broadcasted_iota(jnp.int32, (BR, 1), 0)
    return row < TXT


def unit_and_root(raw):
    wide = raw.astype(F32)
    root = jnp.sqrt(jnp.mean(wide * wide, axis=-1, keepdims=True) + EPS)
    return wide / root, root


def gain_of(mask, gain_ref):
    return jnp.where(mask, gain_ref[0:1, :], gain_ref[1:2, :])


def here():
    return lax.axis_index("zq"), lax.axis_index("zk"), lax.axis_index("x")


def q_block(slot, place):
    zq, zk, x = place
    return (2 * lax.rem(zq + slot, NQ) + zk) * NX + x


def kv_block(xslot, j, place):
    zq, zk, x = place
    return (2 * zq + (zk + j - 2 * zk * j)) * NX + lax.rem(x + xslot, NX)


def q_offset(slot, place):
    return pl.multiple_of(lax.rem(place[0] + slot, NQ) * BR, 16)


def stat_kernel(*refs):
    q_refs, kv_refs = refs[:NQ], refs[NQ : NQ + NX * NZ]
    gq_ref, gk_ref, stat_ref, qn_ref, kn_ref, v_ref, do_ref = refs[NQ + NX * NZ :]
    place = here()
    for slot in range(NQ):
        gain = gain_of(text_mask(q_block(slot, place)), gq_ref)
        rows = pl.ds(q_offset(slot, place), BR)
        for h in range(NH):
            unit, _ = unit_and_root(q_refs[slot][0, h])
            qn_ref[h, rows, :] = (unit * gain).astype(BF16)
            do_ref[h, rows, :] = q_refs[slot][1, h]
    for k in range(NX):
        for j in range(NZ):
            ref = kv_refs[k * NZ + j]
            gain = gain_of(text_mask(kv_block(k, j, place)), gk_ref)
            rows = pl.ds(k * KC + j * BR, BR)
            for h in range(NH):
                unit, _ = unit_and_root(ref[0, h])
                kn_ref[h, rows, :] = (unit * gain).astype(BF16)
                v_ref[h, rows, :] = ref[1, h]
    stat_ref[...] = jnp.zeros_like(stat_ref)
    for h in range(NH):
        top = total = dot = None
        for k in range(NX):
            rows = pl.ds(k * KC, KC)
            s = nt_dot(kn_ref[h, rows, :], qn_ref[h]) * SCALE2
            g = nt_dot(v_ref[h, rows, :], do_ref[h])
            peak = jnp.max(s, axis=0, keepdims=True)
            new = peak if top is None else jnp.maximum(top, peak)
            w = jnp.exp2(s - new)
            part = jnp.sum(w, axis=0, keepdims=True)
            dpart = jnp.sum(w * g, axis=0, keepdims=True)
            if top is None:
                total, dot = part, dpart
            else:
                keep = jnp.exp2(top - new)
                total, dot = total * keep + part, dot * keep + dpart
            top = new
        stat_ref[3 * h : 3 * h + 1, :] = top
        stat_ref[3 * h + 1 : 3 * h + 2, :] = total
        stat_ref[3 * h + 2 : 3 * h + 3, :] = dot


def grad_kernel(*refs):
    s_refs, q_refs = refs[:NQ], refs[NQ : 2 * NQ]
    kv_refs = refs[2 * NQ : 2 * NQ + NX * NZ]
    (gq_ref, gk_ref, qn_ref, kn_ref, v_ref, do_ref,
     dq_own, dq1, dq2, dq3, kv_own, kv1, kv2, kv3, gain_ref, dq_all) = refs[2 * NQ + NX * NZ :]
    place = here()
    kv_outs, dq_outs = (kv_own, kv1, kv2, kv3), (dq_own, dq1, dq2, dq3)
    k_text = jnp.zeros((1, HD), F32)
    k_all = jnp.zeros((1, HD), F32)
    q_text = jnp.zeros((1, HD), F32)
    q_all = jnp.zeros((1, HD), F32)
    for h in range(NH):
        tops = [r[3 * h : 3 * h + 1, :] for r in s_refs]
        top = functools.reduce(jnp.maximum, tops)
        shares = [jnp.exp2(t - top) for t in tops]
        total = sum(r[3 * h + 1 : 3 * h + 2, :] * e for r, e in zip(s_refs, shares))
        row_dot = sum(r[3 * h + 2 : 3 * h + 3, :] * e for r, e in zip(s_refs, shares)) / total
        log_total = top + jnp.log2(total)
        wg = wk = None
        for k in range(NX):
            rows = pl.ds(k * KC, KC)
            kn = kn_ref[h, rows, :]
            s = nt_dot(kn, qn_ref[h]) * SCALE2
            g = nt_dot(v_ref[h, rows, :], do_ref[h])
            p = jnp.exp2(s - log_total)
            low = p.astype(BF16)
            mixed = (p * g).astype(BF16)
            gs = (p * (g - row_dot)).astype(BF16)
            dv = nn_dot(low, do_ref[h])
            dk = nn_dot(gs, qn_ref[h]) * FACTOR
            a, b = tn_dot(mixed, kn), tn_dot(low, kn)
            wg, wk = (a, b) if wg is None else (wg + a, wk + b)
            for j in range(NZ):
                part = dk[j * BR : (j + 1) * BR]
                kv_outs[k][j, 0, h] = part.astype(kv_outs[k].dtype)
                kv_outs[k][j, 1, h] = dv[j * BR : (j + 1) * BR].astype(kv_outs[k].dtype)
                unit, _ = unit_and_root(kv_refs[k * NZ + j][0, h])
                term = part * unit
                k_all += jnp.sum(term, axis=0, keepdims=True)
                k_text += jnp.sum(jnp.where(text_mask(kv_block(k, j, place)), term, 0.0), axis=0, keepdims=True)
        column = jnp.transpose(jnp.broadcast_to(row_dot, (HD, QR)), (1, 0))
        dq_all[...] = (wg - column * wk) * FACTOR
        for slot in range(NQ):
            part = dq_all[pl.ds(q_offset(slot, place), BR), :]
            dq_outs[slot][h] = part.astype(dq_outs[slot].dtype)
            unit, _ = unit_and_root(q_refs[slot][0, h])
            term = part * unit
            q_all += jnp.sum(term, axis=0, keepdims=True)
            q_text += jnp.sum(jnp.where(text_mask(q_block(slot, place)), term, 0.0), axis=0, keepdims=True)
    gain_ref[...] = jnp.concatenate(
        [q_text, q_all - q_text, k_text, k_all - k_text, jnp.zeros((4, HD), F32)], axis=0
    )


def pair_sum_kernel(own, r1, r2, r3, keep_ref, send_ref):
    def total(j):
        return own[j] + r1[j].astype(F32) + r2[j].astype(F32) + r3[j].astype(F32)

    send_ref[...] = total(1).astype(BF16)
    keep_ref[...] = total(0)


def back(grad, raw, gain):
    unit, root = unit_and_root(raw)
    grad = grad * gain
    return (grad - unit * jnp.mean(grad * unit, axis=-1, keepdims=True)) / root


def q_out_kernel(own, r1, r2, r3, raw, gain_ref, out):
    gain = gain_of(text_mask(q_block(0, here())), gain_ref)
    for h in range(NH):
        grad = own[h] + r1[h].astype(F32) + r2[h].astype(F32) + r3[h].astype(F32)
        out[h] = back(grad, raw[0, h], gain).astype(BF16)


def kv_out_kernel(keep, got, raw, gain_ref, k_out, v_out):
    gain = gain_of(text_mask(q_block(0, here())), gain_ref)
    for h in range(NH):
        k_out[h] = back(keep[0, h] + got[0, h].astype(F32), raw[0, h], gain).astype(BF16)
        v_out[h] = (keep[1, h] + got[1, h].astype(F32)).astype(BF16)


def kernel_call(kernel, outs, args, scratch=(), flops=0):
    whole = pl.BlockSpec(memory_space=pltpu.VMEM)
    size = sum(a.size * a.dtype.itemsize for a in args)
    return pl.pallas_call(
        kernel,
        out_shape=[jax.ShapeDtypeStruct(s, d) for s, d in outs],
        in_specs=[whole] * len(args),
        out_specs=[whole] * len(outs),
        scratch_shapes=list(scratch),
        compiler_params=pltpu.CompilerParams(vmem_limit_bytes=48 * 1024 * 1024),
        cost_estimate=pl.CostEstimate(flops=flops, bytes_accessed=size, transcendentals=0),
    )(*args)


def fetch(a, axis, n, k):
    return lax.ppermute(a, axis, [((i + k) % n, i) for i in range(n)])


def give(a, axis, n, k):
    return lax.ppermute(a, axis, [(i, (i + k) % n) for i in range(n)])


def summed(a, axis, n):
    terms = [a] + [lax.ppermute(a, axis, [(i, i ^ k) for i in range(n)]) for k in range(1, n)]
    while len(terms) > 1:
        terms = [terms[i] + terms[i + 1] for i in range(0, len(terms), 2)]
    return terms[0]


def local(q_raw, k_raw, values, out_grad, q_gain, k_gain):
    def heads_first(a):
        return jnp.transpose(a, (1, 0, 2))

    kv = jnp.stack([heads_first(k_raw), heads_first(values)])
    qd = jnp.stack([heads_first(q_raw), heads_first(out_grad)])
    kv_pair = fetch(kv, "zk", NZ, 1)
    kvs = [kv, kv_pair]
    for k in range(1, NX):
        kvs += [fetch(kv, "x", NX, k), fetch(kv_pair, "x", NX, k)]
    qds = [qd] + [fetch(qd, "zq", NQ, k) for k in range(1, NQ)]
    tile = NH * QR * KR * HD * 2
    stat, qn, kn, v, do = kernel_call(
        stat_kernel,
        [((16, QR), F32), ((NH, QR, HD), BF16), ((NH, KR, HD), BF16), ((NH, KR, HD), BF16), ((NH, QR, HD), BF16)],
        [*qds, *kvs, q_gain, k_gain],
        flops=2 * tile,
    )
    stats = [stat] + [fetch(stat, "zq", NQ, k) for k in range(1, NQ)]
    part = (NH, BR, HD)
    kv_part = (NZ, 2, NH, BR, HD)
    dq0, dq1, dq2, dq3, kv0, kv1, kv2, kv3, gains = kernel_call(
        grad_kernel,
        [(part, F32)] + [(part, BF16)] * 3 + [(kv_part, F32)] + [(kv_part, BF16)] * 3 + [((8, HD), F32)],
        [*stats, *qds, *kvs, q_gain, k_gain, qn, kn, v, do],
        scratch=[pltpu.VMEM((QR, HD), F32)],
        flops=6 * tile,
    )
    kv_got = [give(a, "x", NX, k) for k, a in ((1, kv1), (2, kv2), (3, kv3))]
    dq_got = [give(a, "zq", NQ, k) for k, a in ((1, dq1), (2, dq2), (3, dq3))]
    gains = summed(gains, "core", 2)
    gains = summed(gains, "y", 4)
    gains = summed(gains, "x", NX)
    gains = summed(gains, "zk", NZ)
    gains = summed(gains, "zq", NQ)
    keep, send = kernel_call(
        pair_sum_kernel, [((2, NH, BR, HD), F32), ((2, NH, BR, HD), BF16)], [kv0, *kv_got]
    )
    got = fetch(send, "zk", NZ, 1)
    (q_out,) = kernel_call(q_out_kernel, [(part, BF16)], [dq0, *dq_got, qd, q_gain])
    k_out, v_out = kernel_call(kv_out_kernel, [(part, BF16)] * 2, [keep, got, kv, k_gain])

    return (
        heads_first(q_out), heads_first(k_out), heads_first(v_out), gains[0:2], gains[2:4],
    )


def solution(mesh):
    torus = Mesh(mesh.devices.reshape(4, 2, 4, 4, 2), ("zq", "zk", "x", "y", "core"))
    placed = P(ALL_ROWS, ("y", "core"), None)
    return jax.shard_map(
        local,
        mesh=torus,
        in_specs=(placed,) * 4 + (P(), P()),
        out_specs=(placed,) * 3 + (P(), P()),
        check_vma=False,
    )
```

```python
import functools
import math

import jax
import jax.numpy as jnp
from jax import lax
from jax.experimental import pallas as pl
from jax.experimental.pallas import tpu as pltpu
from jax.sharding import Mesh
from jax.sharding import PartitionSpec as P

TXT = 512
EPS = 1e-06
NH, HD, BR = 3, 128, 144
NQ, NX, NZ = 4, 4, 2
QR = NQ * BR
KC = NZ * BR
KR = NX * KC
FACTOR = 1.0 / math.sqrt(HD)
SCALE2 = FACTOR * math.log2(math.e)
F32, BF16 = jnp.float32, jnp.bfloat16
VMEM_LIMIT = 24 * 1024 * 1024
MESSAGE = NH * BR + 32
ALL_ROWS = ("zq", "zk", "x")


def nt_dot(a, b):
    return lax.dot_general(a, b, (((1,), (1,)), ((), ())), preferred_element_type=F32)


def nn_dot(a, b):
    return lax.dot_general(a, b, (((1,), (0,)), ((), ())), preferred_element_type=F32)


def tn_dot(a, b):
    return lax.dot_general(a, b, (((0,), (0,)), ((), ())), preferred_element_type=F32)


def text_mask(block):
    row = block * BR + lax.broadcasted_iota(jnp.int32, (BR, 1), 0)
    return row < TXT


def unit_and_root(raw):
    wide = raw.astype(F32)
    root = jnp.sqrt(jnp.mean(wide * wide, axis=-1, keepdims=True) + EPS)
    return wide / root, root


def gain_of(mask, gain_ref):
    return jnp.where(mask, gain_ref[0:1, :], gain_ref[1:2, :])


def here():
    return lax.axis_index("zq"), lax.axis_index("zk"), lax.axis_index("x")


def q_block(slot, place):
    zq, zk, x = place
    return (2 * (zq ^ slot) + zk) * NX + x


def kv_block(xslot, j, place):
    zq, zk, x = place
    return (2 * zq + (zk + j - 2 * zk * j)) * NX + lax.rem(x + xslot, NX)


def q_offset(slot, place):
    return pl.multiple_of((place[0] ^ slot) * BR, 16)


def stat_kernel(*refs):
    q_refs, kv_refs = refs[:NQ], refs[NQ : NQ + NX * NZ]
    gq_ref, gk_ref, stat_ref, qn_ref, kn_ref, v_ref, do_ref = refs[NQ + NX * NZ :]
    place = here()
    for slot in range(NQ):
        gain = gain_of(text_mask(q_block(slot, place)), gq_ref)
        rows = pl.ds(q_offset(slot, place), BR)
        for h in range(NH):
            unit, _ = unit_and_root(q_refs[slot][0, h])
            qn_ref[h, rows, :] = (unit * gain).astype(BF16)
            do_ref[h, rows, :] = q_refs[slot][1, h]
    for k in range(NX):
        for j in range(NZ):
            ref = kv_refs[k * NZ + j]
            gain = gain_of(text_mask(kv_block(k, j, place)), gk_ref)
            rows = pl.ds(k * KC + j * BR, BR)
            for h in range(NH):
                unit, _ = unit_and_root(ref[0, h])
                kn_ref[h, rows, :] = (unit * gain).astype(BF16)
                v_ref[h, rows, :] = ref[1, h]
    stat_ref[...] = jnp.zeros_like(stat_ref)
    for h in range(NH):
        top = total = dot = None
        for k in range(NX):
            rows = pl.ds(k * KC, KC)
            s = nt_dot(kn_ref[h, rows, :], qn_ref[h]) * SCALE2
            g = nt_dot(v_ref[h, rows, :], do_ref[h])
            peak = jnp.max(s, axis=0, keepdims=True)
            new = peak if top is None else jnp.maximum(top, peak)
            w = jnp.exp2(s - new)
            part = jnp.sum(w, axis=0, keepdims=True)
            dpart = jnp.sum(w * g, axis=0, keepdims=True)
            if top is None:
                total, dot = part, dpart
            else:
                keep = jnp.exp2(top - new)
                total, dot = total * keep + part, dot * keep + dpart
            top = new
        stat_ref[3 * h : 3 * h + 1, :] = top
        stat_ref[3 * h + 1 : 3 * h + 2, :] = total
        stat_ref[3 * h + 2 : 3 * h + 3, :] = dot


def grad_kernel(k, first, last, *refs):
    s_refs, refs = refs[:NQ], refs[NQ:]
    kv_refs, refs = refs[:NZ], refs[NZ:]
    q_refs, refs = (refs[:NQ], refs[NQ:]) if last else ((), refs)
    qn_ref, kn_ref, v_ref, do_ref, *refs = refs
    if first:
        kv_out, dq_ref, gain_ref = refs
    elif last:
        dq_in, gain_in, kv_out, dq0, dq1, dq2, dq3, gain_ref, dq_ref = refs
        dq_outs = (dq0, dq1, dq2, dq3)
    else:
        dq_in, gain_in, kv_out, dq_ref, gain_ref = refs
    place = here()
    k_text = jnp.zeros((1, HD), F32)
    k_all = jnp.zeros((1, HD), F32)
    q_text = jnp.zeros((1, HD), F32)
    q_all = jnp.zeros((1, HD), F32)
    rows = pl.ds(k * KC, KC)
    for h in range(NH):
        tops = [r[3 * h : 3 * h + 1, :] for r in s_refs]
        top = functools.reduce(jnp.maximum, tops)
        shares = [jnp.exp2(t - top) for t in tops]
        total = sum(r[3 * h + 1 : 3 * h + 2, :] * e for r, e in zip(s_refs, shares))
        row_dot = sum(r[3 * h + 2 : 3 * h + 3, :] * e for r, e in zip(s_refs, shares)) / total
        log_total = top + jnp.log2(total)
        kn = kn_ref[h, rows, :]
        s = nt_dot(kn, qn_ref[h]) * SCALE2
        g = nt_dot(v_ref[h, rows, :], do_ref[h])
        p = jnp.exp2(s - log_total)
        low = p.astype(BF16)
        mixed = (p * g).astype(BF16)
        gs = (p * (g - row_dot)).astype(BF16)
        dv = nn_dot(low, do_ref[h])
        dk = nn_dot(gs, qn_ref[h]) * FACTOR
        column = jnp.transpose(jnp.broadcast_to(row_dot, (HD, QR)), (1, 0))
        dq = (tn_dot(mixed, kn) - column * tn_dot(low, kn)) * FACTOR
        dq_ref[h] = dq if first else dq_in[h] + dq
        for j in range(NZ):
            part = dk[j * BR : (j + 1) * BR]
            kv_out[j, 0, h] = part.astype(kv_out.dtype)
            kv_out[j, 1, h] = dv[j * BR : (j + 1) * BR].astype(kv_out.dtype)
            unit, _ = unit_and_root(kv_refs[j][0, h])
            term = part * unit
            k_all += jnp.sum(term, axis=0, keepdims=True)
            k_text += jnp.sum(jnp.where(text_mask(kv_block(k, j, place)), term, 0.0), axis=0, keepdims=True)
        for slot in range(NQ if last else 0):
            part = dq_ref[h, pl.ds(q_offset(slot, place), BR), :]
            dq_outs[slot][h] = part.astype(dq_outs[slot].dtype)
            unit, _ = unit_and_root(q_refs[slot][0, h])
            term = part * unit
            q_all += jnp.sum(term, axis=0, keepdims=True)
            q_text += jnp.sum(jnp.where(text_mask(q_block(slot, place)), term, 0.0), axis=0, keepdims=True)
    gains = jnp.concatenate(
        [q_text, q_all - q_text, k_text, k_all - k_text, jnp.zeros((4, HD), F32)], axis=0
    )
    gain_ref[...] = gains if first else gain_in[...] + gains


def pair_sum_kernel(own, r1, r2, r3, keep_ref, send_ref):
    def total(j):
        return own[j] + r1[j].astype(F32) + r2[j].astype(F32) + r3[j].astype(F32)

    send_ref[...] = total(1).astype(BF16)
    keep_ref[...] = total(0)


def back(grad, raw, gain):
    unit, root = unit_and_root(raw)
    grad = grad * gain
    return (grad - unit * jnp.mean(grad * unit, axis=-1, keepdims=True)) / root


def pack_kernel(dq1, dq2, dq3, gain_ref, m1, m2, m3):
    gains = gain_ref[...]
    high = gains.astype(BF16)
    gains = gains - high.astype(F32)
    middle = gains.astype(BF16)
    low = (gains - middle.astype(F32)).astype(BF16)
    tail = jnp.concatenate([high.astype(F32), middle.astype(F32), low.astype(F32), jnp.zeros((8, HD), F32)], axis=0)
    for dq, out in ((dq1, m1), (dq2, m2), (dq3, m3)):
        for h in range(NH):
            out[h * BR : (h + 1) * BR, :] = dq[h]
        out[NH * BR :, :] = tail.astype(BF16)


def q_out_kernel(own, own_gain, r1, r2, r3, raw, gain_ref, out, sums):
    gain = gain_of(text_mask(q_block(0, here())), gain_ref)
    for h in range(NH):
        rows = slice(h * BR, (h + 1) * BR)
        grad = own[h] + r1[rows, :].astype(F32) + r2[rows, :].astype(F32) + r3[rows, :].astype(F32)
        out[h] = back(grad, raw[0, h], gain).astype(BF16)

    def whole(ref):
        tail = ref[NH * BR :, :].astype(F32)
        return (tail[0:8] + tail[8:16]) + tail[16:24]

    sums[...] = (own_gain[...] + whole(r1)) + (whole(r2) + whole(r3))


def kv_out_kernel(keep, got, raw, gain_ref, k_out, v_out):
    gain = gain_of(text_mask(q_block(0, here())), gain_ref)
    for h in range(NH):
        k_out[h] = back(keep[0, h] + got[0, h].astype(F32), raw[0, h], gain).astype(BF16)
        v_out[h] = (keep[1, h] + got[1, h].astype(F32)).astype(BF16)


def kernel_call(kernel, outs, args, scratch=(), flops=0):
    whole = pl.BlockSpec(memory_space=pltpu.VMEM)
    size = sum(a.size * a.dtype.itemsize for a in args)
    return pl.pallas_call(
        kernel,
        out_shape=[jax.ShapeDtypeStruct(s, d) for s, d in outs],
        in_specs=[whole] * len(args),
        out_specs=[whole] * len(outs),
        scratch_shapes=list(scratch),
        compiler_params=pltpu.CompilerParams(vmem_limit_bytes=VMEM_LIMIT),
        cost_estimate=pl.CostEstimate(flops=flops, bytes_accessed=size, transcendentals=0),
    )(*args)


def fetch(a, axis, n, k):
    return lax.ppermute(a, axis, [((i + k) % n, i) for i in range(n)])


def swap(a, axis, n, k):
    return lax.ppermute(a, axis, [(i, i ^ k) for i in range(n)])


def give(a, axis, n, k):
    return lax.ppermute(a, axis, [(i, (i + k) % n) for i in range(n)])


def summed(a, axis, n):
    terms = [a] + [swap(a, axis, n, k) for k in range(1, n)]
    while len(terms) > 1:
        terms = [terms[i] + terms[i + 1] for i in range(0, len(terms), 2)]
    return terms[0]


def after(a, *others):
    return lax.optimization_barrier((a, *others))[0]


def local(q_raw, k_raw, values, out_grad, q_gain, k_gain):
    def heads_first(a):
        return jnp.transpose(a, (1, 0, 2))

    kv = jnp.stack([heads_first(k_raw), heads_first(values)])
    qd = jnp.stack([heads_first(q_raw), heads_first(out_grad)])
    pair = fetch(kv, "zk", NZ, 1)
    kv_x = [fetch(kv, "x", NX, k) for k in range(1, NX)]
    qd_2 = swap(qd, "zq", NQ, 2)
    pair, qd_now, *_ = lax.optimization_barrier((pair, qd, qd_2, *kv_x))
    kvs = [kv, pair]
    for k in range(1, NX):
        kvs += [kv_x[k - 1], fetch(pair, "x", NX, k)]
    qds = [qd, swap(qd_now, "zq", NQ, 1), qd_2, swap(qd_now, "zq", NQ, 3)]
    tile = NH * QR * KR * HD * 2
    stat, qn, kn, v, do = kernel_call(
        stat_kernel,
        [((16, QR), F32), ((NH, QR, HD), BF16), ((NH, KR, HD), BF16), ((NH, KR, HD), BF16), ((NH, QR, HD), BF16)],
        [*qds, *kvs, q_gain, k_gain],
        flops=2 * tile,
    )
    stats = [stat] + [swap(stat, "zq", NQ, k) for k in range(1, NQ)]
    part = (NH, BR, HD)
    kv_part = (NZ, 2, NH, BR, HD)
    whole_dq, gain_part = ((NH, QR, HD), F32), ((8, HD), F32)
    kv_got, carried = [], []
    for k in (2, 1, 3, 0):
        first, last = k == 2, k == 0
        outs = [(kv_part, F32 if last else BF16)]
        outs += [(part, F32)] + [(part, BF16)] * 3 if last else [whole_dq]
        args = [*stats, *kvs[NZ * k : NZ * k + NZ], *(qds if last else ()), qn, kn, v, do, *carried]
        got = kernel_call(
            functools.partial(grad_kernel, k, first, last),
            outs + [gain_part],
            args,
            scratch=[pltpu.VMEM((NH, QR, HD), F32)] if last else (),
            flops=6 * tile // NX,
        )
        if last:
            own, dq0, dq1, dq2, dq3, gains = got
        else:
            kv_got.append(give(got[0], "x", NX, k))
            carried = got[1:]
    gains = summed(after(gains, kv_got[0]), "core", 2)
    gains = summed(gains, "y", 4)
    gains = summed(after(gains, *kv_got), "x", NX)
    keep, send = kernel_call(
        pair_sum_kernel, [((2, NH, BR, HD), F32), ((2, NH, BR, HD), BF16)], [own, *kv_got]
    )
    got = fetch(send, "zk", NZ, 1)
    gains = after(summed(gains, "zk", NZ), got)
    messages = kernel_call(pack_kernel, [((MESSAGE, HD), BF16)] * 3, [dq1, dq2, dq3, gains])
    messages = [swap(a, "zq", NQ, k) for k, a in enumerate(messages, 1)]
    q_out, gains = kernel_call(
        q_out_kernel, [(part, BF16), ((8, HD), F32)], [dq0, gains, *messages, qd, q_gain]
    )
    k_out, v_out = kernel_call(kv_out_kernel, [(part, BF16)] * 2, [keep, got, kv, k_gain])

    return (
        heads_first(q_out), heads_first(k_out), heads_first(v_out), gains[0:2], gains[2:4],
    )


def solution(mesh):
    torus = Mesh(mesh.devices.reshape(4, 2, 4, 4, 2), ("zq", "zk", "x", "y", "core"))
    placed = P(ALL_ROWS, ("y", "core"), None)
    return jax.shard_map(
        local,
        mesh=torus,
        in_specs=(placed,) * 4 + (P(), P()),
        out_specs=(placed,) * 3 + (P(), P()),
        check_vma=False,
    )
```

```python
import functools
import math

import jax
import jax.numpy as jnp
from jax import lax
from jax.experimental import pallas as pl
from jax.experimental.pallas import tpu as pltpu
from jax.sharding import Mesh
from jax.sharding import PartitionSpec as P

TXT = 512
EPS = 1e-06
NH, HD, BR = 3, 128, 144
NQ, NX, NZ = 4, 4, 2
QR = NQ * BR
KC = NZ * BR
KR = NX * KC
FACTOR = 1.0 / math.sqrt(HD)
SCALE2 = FACTOR * math.log2(math.e)
F32, BF16 = jnp.float32, jnp.bfloat16
VMEM_LIMIT = 24 * 1024 * 1024
MESSAGE = NH * BR + 32
ALL_ROWS = ("zk", "zq", "x")


def nt_dot(a, b):
    return lax.dot_general(a, b, (((1,), (1,)), ((), ())), preferred_element_type=F32)


def nn_dot(a, b):
    return lax.dot_general(a, b, (((1,), (0,)), ((), ())), preferred_element_type=F32)


def tn_dot(a, b):
    return lax.dot_general(a, b, (((0,), (0,)), ((), ())), preferred_element_type=F32)


def text_mask(block):
    row = block * BR + lax.broadcasted_iota(jnp.int32, (BR, 1), 0)
    return row < TXT


def unit_and_root(raw):
    wide = raw.astype(F32)
    root = jnp.sqrt(jnp.mean(wide * wide, axis=-1, keepdims=True) + EPS)
    return wide * (1.0 / root), root


def gain_of(mask, gain_ref):
    return jnp.where(mask, gain_ref[0:1, :], gain_ref[1:2, :])


def here():
    return lax.axis_index("zq"), lax.axis_index("zk"), lax.axis_index("x")


def q_block(slot, place):
    zq, zk, x = place
    return (NQ * zk + (zq ^ slot)) * NX + x


def kv_block(xslot, j, place):
    zq, zk, x = place
    z = NQ * zk + zq
    return ((NQ * NZ - 1 - z) if j else z) * NX + lax.rem(x + xslot, NX)


def q_offset(slot, place):
    return pl.multiple_of((place[0] ^ slot) * BR, 16)


def place_keys(refs, j, gk_ref, kn_ref, v_ref):
    for k in range(NX):
        gain = gain_of(text_mask(kv_block(k, j, here())), gk_ref)
        rows = pl.ds(k * BR, BR)
        for h in range(NH):
            unit, _ = unit_and_root(refs[k][0, h])
            kn_ref[h, rows, :] = (unit * gain).astype(BF16)
            v_ref[h, rows, :] = refs[k][1, h]


def fold_stats(qn_ref, do_ref, kn_ref, v_ref, before_ref, stat_ref):
    for h in range(NH):
        top = total = dot = None
        if before_ref is not None:
            top, total, dot = [before_ref[3 * h + i : 3 * h + i + 1, :] for i in range(3)]
        for at in range(0, NX * BR, KC):
            rows = pl.ds(at, KC)
            s = nt_dot(kn_ref[h, rows, :], qn_ref[h]) * SCALE2
            g = nt_dot(v_ref[h, rows, :], do_ref[h])
            peak = jnp.max(s, axis=0, keepdims=True)
            new = peak if top is None else jnp.maximum(top, peak)
            w = jnp.exp2(s - new)
            part = jnp.sum(w, axis=0, keepdims=True)
            dpart = jnp.sum(w * g, axis=0, keepdims=True)
            if top is None:
                total, dot = part, dpart
            else:
                keep = jnp.exp2(top - new)
                total, dot = total * keep + part, dot * keep + dpart
            top = new
        stat_ref[3 * h : 3 * h + 1, :] = top
        stat_ref[3 * h + 1 : 3 * h + 2, :] = total
        stat_ref[3 * h + 2 : 3 * h + 3, :] = dot


def own_stat_kernel(q0, q1, q2, q3, kv0, kv1, kv2, kv3, gq_ref, gk_ref, stat_ref, qn_ref, do_ref, kn_ref, v_ref):
    place = here()
    for slot, ref in enumerate((q0, q1, q2, q3)):
        gain = gain_of(text_mask(q_block(slot, place)), gq_ref)
        rows = pl.ds(q_offset(slot, place), BR)
        for h in range(NH):
            unit, _ = unit_and_root(ref[0, h])
            qn_ref[h, rows, :] = (unit * gain).astype(BF16)
            do_ref[h, rows, :] = ref[1, h]
    place_keys((kv0, kv1, kv2, kv3), 0, gk_ref, kn_ref, v_ref)
    stat_ref[...] = jnp.zeros_like(stat_ref)
    fold_stats(qn_ref, do_ref, kn_ref, v_ref, None, stat_ref)


def pair_stat_kernel(before_ref, qn_ref, do_ref, kv0, kv1, kv2, kv3, gk_ref, stat_ref, kn_ref, v_ref):
    place_keys((kv0, kv1, kv2, kv3), 1, gk_ref, kn_ref, v_ref)
    stat_ref[...] = jnp.zeros_like(stat_ref)
    fold_stats(qn_ref, do_ref, kn_ref, v_ref, before_ref, stat_ref)


def in_three(sums):
    high = sums.astype(BF16).astype(F32)
    middle = (sums - high).astype(BF16).astype(F32)
    low = ((sums - high) - middle).astype(BF16).astype(F32)
    tail = jnp.concatenate([high, middle, low, jnp.zeros_like(sums)], axis=0).astype(BF16)
    return tail, (high + middle) + low


def grad_kernel(k, first, last, *refs):
    s_refs, refs = refs[:NQ], refs[NQ:]
    kv_refs, refs = refs[:NZ], refs[NZ:]
    q_refs, refs = (refs[:NQ], refs[NQ:]) if last else ((), refs)
    qn_ref, do_ref, kn_own, v_own, kn_pair, v_pair, *refs = refs
    if first:
        kv_out, dq_ref, gain_ref = refs
    elif last:
        dq_in, gain_in, kv_out, dq_own, *messages, gain_ref, dq_ref = refs
    else:
        dq_in, gain_in, kv_out, dq_ref, gain_ref = refs
    place = here()
    k_text = jnp.zeros((1, HD), F32)
    k_all = jnp.zeros((1, HD), F32)
    q_text = jnp.zeros((1, HD), F32)
    q_all = jnp.zeros((1, HD), F32)
    rows = pl.ds(k * BR, BR)
    for h in range(NH):
        tops = [r[3 * h : 3 * h + 1, :] for r in s_refs]
        top = functools.reduce(jnp.maximum, tops)
        shares = [jnp.exp2(t - top) for t in tops]
        total = sum(r[3 * h + 1 : 3 * h + 2, :] * e for r, e in zip(s_refs, shares))
        row_dot = sum(r[3 * h + 2 : 3 * h + 3, :] * e for r, e in zip(s_refs, shares)) / total
        log_total = top + jnp.log2(total)
        kn = jnp.concatenate([kn_own[h, rows, :], kn_pair[h, rows, :]], axis=0)
        v = jnp.concatenate([v_own[h, rows, :], v_pair[h, rows, :]], axis=0)
        s = nt_dot(kn, qn_ref[h]) * SCALE2
        g = nt_dot(v, do_ref[h])
        p = jnp.exp2(s - log_total)
        low = p.astype(BF16)
        mixed = (p * g).astype(BF16)
        gs = (p * (g - row_dot)).astype(BF16)
        dv = nn_dot(low, do_ref[h])
        dk = nn_dot(gs, qn_ref[h]) * FACTOR
        dq = (tn_dot(kn, mixed) - row_dot * tn_dot(kn, low)) * FACTOR
        dq = jnp.transpose(dq, (1, 0))
        dq_ref[h] = dq if first else dq_in[h] + dq
        for j in range(NZ):
            part = dk[j * BR : (j + 1) * BR]
            kv_out[j, 0, h] = part.astype(kv_out.dtype)
            kv_out[j, 1, h] = dv[j * BR : (j + 1) * BR].astype(kv_out.dtype)
            unit, _ = unit_and_root(kv_refs[j][0, h])
            term = part * unit
            k_all += jnp.sum(term, axis=0, keepdims=True)
            k_text += jnp.sum(jnp.where(text_mask(kv_block(k, j, place)), term, 0.0), axis=0, keepdims=True)
        for slot in range(NQ if last else 0):
            part = dq_ref[h, pl.ds(q_offset(slot, place), BR), :]
            if slot == 0:
                dq_own[h] = part
            else:
                messages[slot - 1][h * BR : (h + 1) * BR, :] = part.astype(BF16)
            unit, _ = unit_and_root(q_refs[slot][0, h])
            term = part * unit
            q_all += jnp.sum(term, axis=0, keepdims=True)
            q_text += jnp.sum(jnp.where(text_mask(q_block(slot, place)), term, 0.0), axis=0, keepdims=True)
    gains = jnp.concatenate(
        [q_text, q_all - q_text, k_text, k_all - k_text, jnp.zeros((4, HD), F32)], axis=0
    )
    gains = gains if first else gain_in[...] + gains
    if last:
        tail, gains = in_three(gains)
        for out in messages:
            out[NH * BR :, :] = tail
    gain_ref[...] = gains


def pair_sum_kernel(own, r1, r2, r3, keep_ref, send_k, send_v):
    def total(j, i):
        return own[j, i] + r1[j, i].astype(F32) + r2[j, i].astype(F32) + r3[j, i].astype(F32)

    for i, send in ((0, send_k), (1, send_v)):
        send[...] = total(1, i).astype(BF16)
        keep_ref[i] = total(0, i)


def back(grad, raw, gain):
    unit, root = unit_and_root(raw)
    grad = grad * gain
    return (grad - unit * jnp.mean(grad * unit, axis=-1, keepdims=True)) * (1.0 / root)


def q_out_kernel(own, own_gain, r1, r2, r3, raw, gain_ref, out, sums):
    gain = gain_of(text_mask(q_block(0, here())), gain_ref)
    for h in range(NH):
        rows = slice(h * BR, (h + 1) * BR)
        grad = own[h] + r1[rows, :].astype(F32) + r2[rows, :].astype(F32) + r3[rows, :].astype(F32)
        out[h] = back(grad, raw[0, h], gain).astype(BF16)

    def whole(ref):
        tail = ref[NH * BR :, :].astype(F32)
        return (tail[0:8] + tail[8:16]) + tail[16:24]

    sums[...] = (own_gain[...] + whole(r1)) + (whole(r2) + whole(r3))


def kv_out_kernel(keep, got_k, got_v, raw, gain_ref, k_out, v_out):
    gain = gain_of(text_mask(q_block(0, here())), gain_ref)
    for h in range(NH):
        k_out[h] = back(keep[0, h] + got_k[h].astype(F32), raw[0, h], gain).astype(BF16)
        v_out[h] = (keep[1, h] + got_v[h].astype(F32)).astype(BF16)


def kernel_call(kernel, outs, args, scratch=(), flops=0):
    whole = pl.BlockSpec(memory_space=pltpu.VMEM)
    size = sum(a.size * a.dtype.itemsize for a in args)
    return pl.pallas_call(
        kernel,
        out_shape=[jax.ShapeDtypeStruct(s, d) for s, d in outs],
        in_specs=[whole] * len(args),
        out_specs=[whole] * len(outs),
        scratch_shapes=list(scratch),
        compiler_params=pltpu.CompilerParams(vmem_limit_bytes=VMEM_LIMIT),
        cost_estimate=pl.CostEstimate(flops=flops, bytes_accessed=size, transcendentals=0),
    )(*args)


def fetch(a, axis, n, k):
    return lax.ppermute(a, axis, [((i + k) % n, i) for i in range(n)])


def swap(a, axis, n, k):
    return lax.ppermute(a, axis, [(i, i ^ k) for i in range(n)])


def give(a, axis, n, k):
    return lax.ppermute(a, axis, [(i, (i + k) % n) for i in range(n)])


def mirror(a):
    n = NZ * NQ
    return lax.ppermute(a, ("zk", "zq"), [(i, n - 1 - i) for i in range(n)])


def summed(a, axis, n, *others):
    terms = [a] + [swap(a, axis, n, k) for k in range(1, n)]
    terms = lax.optimization_barrier((*terms, *others))[:n]
    return (terms[0] + terms[1]) + (terms[2] + terms[3])


def after(a, *others):
    return lax.optimization_barrier((a, *others))[0]


def local(q_raw, k_raw, values, out_grad, q_gain, k_gain):
    def heads_first(a):
        return jnp.transpose(a, (1, 0, 2))

    kv = jnp.stack([heads_first(k_raw), heads_first(values)])
    qd = jnp.stack([heads_first(q_raw), heads_first(out_grad)])
    pair = mirror(kv)
    x1, x2, x3 = [fetch(kv, "x", NX, k) for k in range(1, NX)]
    q3 = swap(qd, "zq", NQ, 3)
    q2 = swap(after(qd, q3), "zq", NQ, 2)
    x1, x3, x2, pair, qd_now = lax.optimization_barrier((x1, x3, x2, pair, qd))
    p1, p2, p3 = [fetch(pair, "x", NX, k) for k in range(1, NX)]
    q1 = swap(qd_now, "zq", NQ, 1)
    kvs = [kv, pair, x1, p1, x2, p2, x3, p3]
    qds = [qd, q1, q2, q3]
    tile = NH * QR * KR * HD * 2
    stat_shape, q_shape, k_shape = ((16, QR), F32), ((NH, QR, HD), BF16), ((NH, NX * BR, HD), BF16)
    stat, qn, do, kn_own, v_own = kernel_call(
        own_stat_kernel,
        [stat_shape, q_shape, q_shape, k_shape, k_shape],
        [*qds, kv, x1, x2, x3, q_gain, k_gain],
        flops=tile,
    )
    stat, kn_pair, v_pair = kernel_call(
        pair_stat_kernel,
        [stat_shape, k_shape, k_shape],
        [stat, qn, do, pair, p1, p2, p3, k_gain],
        flops=tile,
    )
    stats = [stat] + [swap(stat, "zq", NQ, k) for k in (1, 2, 3)]
    part = (NH, BR, HD)
    kv_part = (NZ, 2, NH, BR, HD)
    whole_dq, gain_part = ((NH, QR, HD), F32), ((8, HD), F32)
    kv_got, carried = [], []
    for k in (2, 1, 3, 0):
        first, last = k == 2, k == 0
        outs = [(kv_part, F32 if last else BF16)]
        outs += [(part, F32)] + [((MESSAGE, HD), BF16)] * 3 if last else [whole_dq]
        args = [*stats, *kvs[NZ * k : NZ * k + NZ], *(qds if last else ()), qn, do, kn_own, v_own, kn_pair, v_pair, *carried]
        got = kernel_call(
            functools.partial(grad_kernel, k, first, last),
            outs + [gain_part],
            args,
            scratch=[pltpu.VMEM((NH, QR, HD), F32)] if last else (),
            flops=6 * tile // NX,
        )
        if last:
            own, dq_own, *messages, gains = got
        else:
            kv_got.append(give(got[0], "x", NX, k))
            carried = got[1:]
    m1, m2, m3 = messages
    m2 = swap(after(m2, kv_got[0]), "zq", NQ, 2)
    m1, m3 = swap(m1, "zq", NQ, 1), swap(m3, "zq", NQ, 3)
    q_out, gains = kernel_call(
        q_out_kernel, [(part, BF16), ((8, HD), F32)], [dq_own, gains, m1, m2, m3, qd, q_gain]
    )
    gains = gains + swap(gains, "core", 2, 1)
    gains = gains + mirror(gains)
    keep, send_k, send_v = kernel_call(
        pair_sum_kernel, [((2, NH, BR, HD), F32), (part, BF16), (part, BF16)], [own, *kv_got]
    )
    got_k = mirror(send_k)
    gains = summed(after(gains, send_k), "y", 4, got_k)
    gains = summed(gains, "x", NX)
    k_out, v_out = kernel_call(
        kv_out_kernel, [(part, BF16)] * 2, [keep, got_k, mirror(send_v), kv, k_gain]
    )

    return (
        heads_first(q_out), heads_first(k_out), heads_first(v_out), gains[0:2], gains[2:4],
    )


def solution(mesh):
    torus = Mesh(mesh.devices.reshape(2, 4, 4, 4, 2), ("zk", "zq", "x", "y", "core"))
    placed = P(ALL_ROWS, ("y", "core"), None)
    return jax.shard_map(
        local,
        mesh=torus,
        in_specs=(placed,) * 4 + (P(), P()),
        out_specs=(placed,) * 3 + (P(), P()),
        check_vma=False,
    )
```

```python
import functools
import math

import jax
import jax.numpy as jnp
from jax import lax
from jax.experimental import pallas as pl
from jax.experimental.pallas import tpu as pltpu
from jax.sharding import Mesh
from jax.sharding import PartitionSpec as P

TXT = 512
EPS = 1e-06
NH, HD, BR = 3, 128, 144
NQ, NX, NZ = 4, 4, 2
QR = NQ * BR
KC = NZ * BR
KR = NX * KC
FACTOR = 1.0 / math.sqrt(HD)
SCALE2 = FACTOR * math.log2(math.e)
F32, BF16 = jnp.float32, jnp.bfloat16
VMEM_LIMIT = 24 * 1024 * 1024
ALL_ROWS = ("zk", "zq", "x")


def nt_dot(a, b):
    return lax.dot_general(a, b, (((1,), (1,)), ((), ())), preferred_element_type=F32)


def nn_dot(a, b):
    return lax.dot_general(a, b, (((1,), (0,)), ((), ())), preferred_element_type=F32)


def tn_dot(a, b):
    return lax.dot_general(a, b, (((0,), (0,)), ((), ())), preferred_element_type=F32)


def text_mask(block):
    row = block * BR + lax.broadcasted_iota(jnp.int32, (BR, 1), 0)
    return row < TXT


def unit_and_root(raw):
    wide = raw.astype(F32)
    root = jnp.sqrt(jnp.mean(wide * wide, axis=-1, keepdims=True) + EPS)
    return wide * (1.0 / root), root


def gain_of(mask, gain_ref):
    return jnp.where(mask, gain_ref[0:1, :], gain_ref[1:2, :])


def here():
    return lax.axis_index("zq"), lax.axis_index("zk"), lax.axis_index("x")


def q_block(slot, place):
    zq, zk, x = place
    return (NQ * zk + (zq ^ slot)) * NX + x


def kv_block(xslot, j, place):
    zq, zk, x = place
    z = NQ * zk + zq
    return ((NQ * NZ - 1 - z) if j else z) * NX + lax.rem(x + xslot, NX)


def q_offset(slot, place):
    return pl.multiple_of((place[0] ^ slot) * BR, 16)


def place_keys(refs, j, gk_ref, kn_ref, v_ref):
    for k in range(NX):
        gain = gain_of(text_mask(kv_block(k, j, here())), gk_ref)
        rows = pl.ds(k * BR, BR)
        for h in range(NH):
            unit, _ = unit_and_root(refs[k][0, h])
            kn_ref[h, rows, :] = (unit * gain).astype(BF16)
            v_ref[h, rows, :] = refs[k][1, h]


def fold_stats(qn_ref, do_ref, kn_ref, v_ref, before_ref, stat_ref):
    for h in range(NH):
        top = total = dot = None
        if before_ref is not None:
            top, total, dot = [before_ref[3 * h + i : 3 * h + i + 1, :] for i in range(3)]
        for at in range(0, NX * BR, KC):
            rows = pl.ds(at, KC)
            s = nt_dot(kn_ref[h, rows, :], qn_ref[h]) * SCALE2
            g = nt_dot(v_ref[h, rows, :], do_ref[h])
            peak = jnp.max(s, axis=0, keepdims=True)
            new = peak if top is None else jnp.maximum(top, peak)
            w = jnp.exp2(s - new)
            part = jnp.sum(w, axis=0, keepdims=True)
            dpart = jnp.sum(w * g, axis=0, keepdims=True)
            if top is None:
                total, dot = part, dpart
            else:
                keep = jnp.exp2(top - new)
                total, dot = total * keep + part, dot * keep + dpart
            top = new
        stat_ref[3 * h : 3 * h + 1, :] = top
        stat_ref[3 * h + 1 : 3 * h + 2, :] = total
        stat_ref[3 * h + 2 : 3 * h + 3, :] = dot


def own_stat_kernel(q0, q1, q2, q3, kv0, kv1, kv2, kv3, gq_ref, gk_ref, stat_ref, qn_ref, do_ref, kn_ref, v_ref):
    place = here()
    for slot, ref in enumerate((q0, q1, q2, q3)):
        gain = gain_of(text_mask(q_block(slot, place)), gq_ref)
        rows = pl.ds(q_offset(slot, place), BR)
        for h in range(NH):
            unit, _ = unit_and_root(ref[0, h])
            qn_ref[h, rows, :] = (unit * gain).astype(BF16)
            do_ref[h, rows, :] = ref[1, h]
    place_keys((kv0, kv1, kv2, kv3), 0, gk_ref, kn_ref, v_ref)
    stat_ref[...] = jnp.zeros_like(stat_ref)
    fold_stats(qn_ref, do_ref, kn_ref, v_ref, None, stat_ref)


def pair_stat_kernel(before_ref, qn_ref, do_ref, kv0, kv1, kv2, kv3, gk_ref, stat_ref, kn_ref, v_ref):
    place_keys((kv0, kv1, kv2, kv3), 1, gk_ref, kn_ref, v_ref)
    stat_ref[...] = jnp.zeros_like(stat_ref)
    fold_stats(qn_ref, do_ref, kn_ref, v_ref, before_ref, stat_ref)


def grad_kernel(k, first, last, *refs):
    s_refs, refs = refs[:NQ], refs[NQ:]
    kv_refs, refs = refs[:NZ], refs[NZ:]
    q_refs, refs = (refs[:NQ], refs[NQ:]) if last else ((), refs)
    qn_ref, do_ref, kn_own, v_own, kn_pair, v_pair, *refs = refs
    if first:
        kv_out, dq_ref, gain_ref = refs
    elif last:
        dq_in, gain_in, kv_out, dq_own, *messages, gain_ref, dq_ref = refs
    else:
        dq_in, gain_in, kv_out, dq_ref, gain_ref = refs
    place = here()
    k_text = jnp.zeros((1, HD), F32)
    k_all = jnp.zeros((1, HD), F32)
    q_text = jnp.zeros((1, HD), F32)
    q_all = jnp.zeros((1, HD), F32)
    rows = pl.ds(k * BR, BR)
    for h in range(NH):
        tops = [r[3 * h : 3 * h + 1, :] for r in s_refs]
        top = functools.reduce(jnp.maximum, tops)
        shares = [jnp.exp2(t - top) for t in tops]
        total = sum(r[3 * h + 1 : 3 * h + 2, :] * e for r, e in zip(s_refs, shares))
        row_dot = sum(r[3 * h + 2 : 3 * h + 3, :] * e for r, e in zip(s_refs, shares)) / total
        log_total = top + jnp.log2(total)
        kn = jnp.concatenate([kn_own[h, rows, :], kn_pair[h, rows, :]], axis=0)
        v = jnp.concatenate([v_own[h, rows, :], v_pair[h, rows, :]], axis=0)
        s = nt_dot(kn, qn_ref[h]) * SCALE2
        g = nt_dot(v, do_ref[h])
        p = jnp.exp2(s - log_total)
        low = p.astype(BF16)
        mixed = (p * g).astype(BF16)
        gs = (p * (g - row_dot)).astype(BF16)
        dv = nn_dot(low, do_ref[h])
        dk = nn_dot(gs, qn_ref[h]) * FACTOR
        dq = (tn_dot(kn, mixed) - row_dot * tn_dot(kn, low)) * FACTOR
        dq = jnp.transpose(dq, (1, 0))
        dq_ref[h] = dq if first else dq_in[h] + dq
        for j in range(NZ):
            part = dk[j * BR : (j + 1) * BR]
            kv_out[j, 0, h] = part.astype(kv_out.dtype)
            kv_out[j, 1, h] = dv[j * BR : (j + 1) * BR].astype(kv_out.dtype)
            unit, _ = unit_and_root(kv_refs[j][0, h])
            term = part * unit
            k_all += jnp.sum(term, axis=0, keepdims=True)
            k_text += jnp.sum(jnp.where(text_mask(kv_block(k, j, place)), term, 0.0), axis=0, keepdims=True)
        for slot in range(NQ if last else 0):
            part = dq_ref[h, pl.ds(q_offset(slot, place), BR), :]
            if slot == 0:
                dq_own[h] = part
            else:
                messages[slot - 1][h] = part.astype(BF16)
            unit, _ = unit_and_root(q_refs[slot][0, h])
            term = part * unit
            q_all += jnp.sum(term, axis=0, keepdims=True)
            q_text += jnp.sum(jnp.where(text_mask(q_block(slot, place)), term, 0.0), axis=0, keepdims=True)
    gains = jnp.concatenate(
        [q_text, q_all - q_text, k_text, k_all - k_text, jnp.zeros((4, HD), F32)], axis=0
    )
    gains = gains if first else gain_in[...] + gains
    gain_ref[...] = gains


def pair_sum_kernel(own, r1, r2, r3, keep_ref, send_ref):
    def total(j, i):
        return own[j, i] + r1[j, i].astype(F32) + r2[j, i].astype(F32) + r3[j, i].astype(F32)

    for i in range(2):
        send_ref[i] = total(1, i).astype(BF16)
        keep_ref[i] = total(0, i)


def back(grad, raw, gain):
    unit, root = unit_and_root(raw)
    grad = grad * gain
    return (grad - unit * jnp.mean(grad * unit, axis=-1, keepdims=True)) * (1.0 / root)


def q_out_kernel(own, r1, r2, r3, raw, gain_ref, out):
    gain = gain_of(text_mask(q_block(0, here())), gain_ref)
    for h in range(NH):
        grad = own[h] + r1[h].astype(F32) + r2[h].astype(F32) + r3[h].astype(F32)
        out[h] = back(grad, raw[0, h], gain).astype(BF16)


def kv_out_kernel(keep, got, raw, gain_ref, k_out, v_out):
    gain = gain_of(text_mask(q_block(0, here())), gain_ref)
    for h in range(NH):
        k_out[h] = back(keep[0, h] + got[0, h].astype(F32), raw[0, h], gain).astype(BF16)
        v_out[h] = (keep[1, h] + got[1, h].astype(F32)).astype(BF16)


def kernel_call(kernel, outs, args, scratch=(), flops=0):
    whole = pl.BlockSpec(memory_space=pltpu.VMEM)
    size = sum(a.size * a.dtype.itemsize for a in args)
    return pl.pallas_call(
        kernel,
        out_shape=[jax.ShapeDtypeStruct(s, d) for s, d in outs],
        in_specs=[whole] * len(args),
        out_specs=[whole] * len(outs),
        scratch_shapes=list(scratch),
        compiler_params=pltpu.CompilerParams(vmem_limit_bytes=VMEM_LIMIT),
        cost_estimate=pl.CostEstimate(flops=flops, bytes_accessed=size, transcendentals=0),
    )(*args)


def fetch(a, axis, n, k):
    return lax.ppermute(a, axis, [((i + k) % n, i) for i in range(n)])


def swap(a, axis, n, k):
    return lax.ppermute(a, axis, [(i, i ^ k) for i in range(n)])


def give(a, axis, n, k):
    return lax.ppermute(a, axis, [(i, (i + k) % n) for i in range(n)])


def mirror(a):
    n = NZ * NQ
    return lax.ppermute(a, ("zk", "zq"), [(i, n - 1 - i) for i in range(n)])


def summed(a, axis, n, *others):
    terms = [a] + [swap(a, axis, n, k) for k in range(1, n)]
    terms = lax.optimization_barrier((*terms, *others))[:n]
    return (terms[0] + terms[1]) + (terms[2] + terms[3])


def after(a, *others):
    return lax.optimization_barrier((a, *others))[0]


def local(q_raw, k_raw, values, out_grad, q_gain, k_gain):
    def heads_first(a):
        return jnp.transpose(a, (1, 0, 2))

    kv = jnp.stack([heads_first(k_raw), heads_first(values)])
    qd = jnp.stack([heads_first(q_raw), heads_first(out_grad)])
    pair = mirror(kv)
    x1, x2, x3 = [fetch(kv, "x", NX, k) for k in range(1, NX)]
    q3 = swap(qd, "zq", NQ, 3)
    q2 = swap(after(qd, q3), "zq", NQ, 2)
    x1, x3, x2, pair, qd_now = lax.optimization_barrier((x1, x3, x2, pair, qd))
    p1, p2, p3 = [fetch(pair, "x", NX, k) for k in range(1, NX)]
    q1 = swap(qd_now, "zq", NQ, 1)
    kvs = [kv, pair, x1, p1, x2, p2, x3, p3]
    qds = [qd, q1, q2, q3]
    tile = NH * QR * KR * HD * 2
    stat_shape, q_shape, k_shape = ((16, QR), F32), ((NH, QR, HD), BF16), ((NH, NX * BR, HD), BF16)
    stat, qn, do, kn_own, v_own = kernel_call(
        own_stat_kernel,
        [stat_shape, q_shape, q_shape, k_shape, k_shape],
        [*qds, kv, x1, x2, x3, q_gain, k_gain],
        flops=tile,
    )
    stat, kn_pair, v_pair = kernel_call(
        pair_stat_kernel,
        [stat_shape, k_shape, k_shape],
        [stat, qn, do, pair, p1, p2, p3, k_gain],
        flops=tile,
    )
    stats = [stat] + [swap(stat, "zq", NQ, k) for k in (1, 2, 3)]
    part = (NH, BR, HD)
    kv_part = (NZ, 2, NH, BR, HD)
    whole_dq, gain_part = ((NH, QR, HD), F32), ((8, HD), F32)
    kv_got, carried = [], []
    for k in (2, 1, 3, 0):
        first, last = k == 2, k == 0
        outs = [(kv_part, F32 if last else BF16)]
        outs += [(part, F32)] + [(part, BF16)] * 3 if last else [whole_dq]
        args = [*stats, *kvs[NZ * k : NZ * k + NZ], *(qds if last else ()), qn, do, kn_own, v_own, kn_pair, v_pair, *carried]
        got = kernel_call(
            functools.partial(grad_kernel, k, first, last),
            outs + [gain_part],
            args,
            scratch=[pltpu.VMEM((NH, QR, HD), F32)] if last else (),
            flops=6 * tile // NX,
        )
        if last:
            own, dq_own, *messages, gains = got
        else:
            kv_got.append(give(got[0], "x", NX, k))
            carried = got[1:]
    gains = summed(gains, "zq", NQ, kv_got[0])
    messages = [swap(m, "zq", NQ, k) for k, m in enumerate(messages, 1)]
    gains = gains + swap(gains, "core", 2, 1)
    gains = gains + mirror(gains)
    keep, send = kernel_call(
        pair_sum_kernel, [((2, NH, BR, HD), F32), ((2, NH, BR, HD), BF16)], [own, *kv_got]
    )
    got = mirror(send)
    gains = summed(gains, "y", 4, *messages)
    (q_out,) = kernel_call(q_out_kernel, [(part, BF16)], [dq_own, *messages, qd, q_gain])
    gains = summed(after(gains, send), "x", NX, got)
    k_out, v_out = kernel_call(
        kv_out_kernel, [(part, BF16)] * 2, [keep, got, kv, k_gain]
    )

    return (
        heads_first(q_out), heads_first(k_out), heads_first(v_out), gains[0:2], gains[2:4],
    )


def solution(mesh):
    torus = Mesh(mesh.devices.reshape(2, 4, 4, 4, 2), ("zk", "zq", "x", "y", "core"))
    placed = P(ALL_ROWS, ("y", "core"), None)
    return jax.shard_map(
        local,
        mesh=torus,
        in_specs=(placed,) * 4 + (P(), P()),
        out_specs=(placed,) * 3 + (P(), P()),
        check_vma=False,
    )
```

```python
import functools
import math

import jax
import jax.numpy as jnp
from jax import lax
from jax.experimental import pallas as pl
from jax.experimental.pallas import tpu as pltpu
from jax.sharding import Mesh
from jax.sharding import PartitionSpec as P

TXT = 512
EPS = 1e-06
NH, HD, BR = 3, 128, 144
NQ, NX, NZ = 4, 4, 2
QR = NQ * BR
KC = NZ * BR
KR = NX * KC
FACTOR = 1.0 / math.sqrt(HD)
SCALE2 = FACTOR * math.log2(math.e)
F32, BF16 = jnp.float32, jnp.bfloat16
VMEM_LIMIT = 24 * 1024 * 1024
ALL_ROWS = ("zk", "zq", "x")


def nt_dot(a, b):
    return lax.dot_general(a, b, (((1,), (1,)), ((), ())), preferred_element_type=F32)


def nn_dot(a, b):
    return lax.dot_general(a, b, (((1,), (0,)), ((), ())), preferred_element_type=F32)


def tn_dot(a, b):
    return lax.dot_general(a, b, (((0,), (0,)), ((), ())), preferred_element_type=F32)


def text_mask(block):
    row = block * BR + lax.broadcasted_iota(jnp.int32, (BR, 1), 0)
    return row < TXT


def unit_and_root(raw):
    wide = raw.astype(F32)
    root = jnp.sqrt(jnp.mean(wide * wide, axis=-1, keepdims=True) + EPS)
    return wide * (1.0 / root), root


def gain_of(mask, gain_ref):
    return jnp.where(mask, gain_ref[0:1, :], gain_ref[1:2, :])


def here():
    return lax.axis_index("zq"), lax.axis_index("zk"), lax.axis_index("x")


def q_block(slot, place):
    zq, zk, x = place
    return (NQ * zk + (zq ^ slot)) * NX + x


def kv_block(xslot, j, place):
    zq, zk, x = place
    z = NQ * zk + zq
    return ((NQ * NZ - 1 - z) if j else z) * NX + lax.rem(x + xslot, NX)


def q_offset(slot, place):
    return pl.multiple_of((place[0] ^ slot) * BR, 16)


def place_keys(refs, slots, j, gk_ref, kn_ref, v_ref):
    for at, (k, ref) in enumerate(zip(slots, refs)):
        gain = gain_of(text_mask(kv_block(k, j, here())), gk_ref)
        rows = pl.ds(at * BR, BR)
        for h in range(NH):
            unit, _ = unit_and_root(ref[0, h])
            kn_ref[h, rows, :] = (unit * gain).astype(BF16)
            v_ref[h, rows, :] = ref[1, h]


def fold_stats(qn_ref, do_ref, kn_ref, v_ref, before_ref, stat_ref):
    for h in range(NH):
        top = total = dot = None
        if before_ref is not None:
            top, total, dot = [before_ref[3 * h + i : 3 * h + i + 1, :] for i in range(3)]
        for at in range(0, kn_ref.shape[1], KC):
            rows = pl.ds(at, KC)
            s = nt_dot(kn_ref[h, rows, :], qn_ref[h]) * SCALE2
            g = nt_dot(v_ref[h, rows, :], do_ref[h])
            peak = jnp.max(s, axis=0, keepdims=True)
            new = peak if top is None else jnp.maximum(top, peak)
            w = jnp.exp2(s - new)
            part = jnp.sum(w, axis=0, keepdims=True)
            dpart = jnp.sum(w * g, axis=0, keepdims=True)
            if top is None:
                total, dot = part, dpart
            else:
                keep = jnp.exp2(top - new)
                total, dot = total * keep + part, dot * keep + dpart
            top = new
        stat_ref[3 * h : 3 * h + 1, :] = top
        stat_ref[3 * h + 1 : 3 * h + 2, :] = total
        stat_ref[3 * h + 2 : 3 * h + 3, :] = dot


def own_stat_kernel(q0, q1, q2, q3, kv0, kv1, kv2, kv3, gq_ref, gk_ref, stat_ref, qn_ref, do_ref, kn_ref, v_ref):
    place = here()
    for slot, ref in enumerate((q0, q1, q2, q3)):
        gain = gain_of(text_mask(q_block(slot, place)), gq_ref)
        rows = pl.ds(q_offset(slot, place), BR)
        for h in range(NH):
            unit, _ = unit_and_root(ref[0, h])
            qn_ref[h, rows, :] = (unit * gain).astype(BF16)
            do_ref[h, rows, :] = ref[1, h]
    place_keys((kv0, kv1, kv2, kv3), range(NX), 0, gk_ref, kn_ref, v_ref)
    stat_ref[...] = jnp.zeros_like(stat_ref)
    fold_stats(qn_ref, do_ref, kn_ref, v_ref, None, stat_ref)


def pair_stat_kernel(slots, before_ref, qn_ref, do_ref, kv_a, kv_b, gk_ref, stat_ref, kn_ref, v_ref):
    place_keys((kv_a, kv_b), slots, 1, gk_ref, kn_ref, v_ref)
    stat_ref[...] = jnp.zeros_like(stat_ref)
    fold_stats(qn_ref, do_ref, kn_ref, v_ref, before_ref, stat_ref)


def grad_kernel(k, first, last, *refs):
    s_refs, refs = refs[:NQ], refs[NQ:]
    kv_refs, refs = refs[:NZ], refs[NZ:]
    q_refs, refs = (refs[:NQ], refs[NQ:]) if last else ((), refs)
    qn_ref, do_ref, kn_own, v_own, kn_pair, v_pair, *refs = refs
    if first:
        kv_out, dq_ref, gain_ref = refs
    elif last:
        dq_in, gain_in, kv_out, dq_own, *messages, gain_ref, dq_ref = refs
    else:
        dq_in, gain_in, kv_out, dq_ref, gain_ref = refs
    place = here()
    k_text = jnp.zeros((1, HD), F32)
    k_all = jnp.zeros((1, HD), F32)
    q_text = jnp.zeros((1, HD), F32)
    q_all = jnp.zeros((1, HD), F32)
    rows, pair_rows = pl.ds(k * BR, BR), pl.ds(k // 2 * BR, BR)
    for h in range(NH):
        tops = [r[3 * h : 3 * h + 1, :] for r in s_refs]
        top = functools.reduce(jnp.maximum, tops)
        shares = [jnp.exp2(t - top) for t in tops]
        total = sum(r[3 * h + 1 : 3 * h + 2, :] * e for r, e in zip(s_refs, shares))
        row_dot = sum(r[3 * h + 2 : 3 * h + 3, :] * e for r, e in zip(s_refs, shares)) / total
        log_total = top + jnp.log2(total)
        kn = jnp.concatenate([kn_own[h, rows, :], kn_pair[h, pair_rows, :]], axis=0)
        v = jnp.concatenate([v_own[h, rows, :], v_pair[h, pair_rows, :]], axis=0)
        s = nt_dot(kn, qn_ref[h]) * SCALE2
        g = nt_dot(v, do_ref[h])
        p = jnp.exp2(s - log_total)
        low = p.astype(BF16)
        mixed = (p * g).astype(BF16)
        gs = (p * (g - row_dot)).astype(BF16)
        dv = nn_dot(low, do_ref[h])
        dk = nn_dot(gs, qn_ref[h]) * FACTOR
        dq = (tn_dot(kn, mixed) - row_dot * tn_dot(kn, low)) * FACTOR
        dq = jnp.transpose(dq, (1, 0))
        dq_ref[h] = dq if first else dq_in[h] + dq
        for j in range(NZ):
            part = dk[j * BR : (j + 1) * BR]
            kv_out[j, 0, h] = part.astype(kv_out.dtype)
            kv_out[j, 1, h] = dv[j * BR : (j + 1) * BR].astype(kv_out.dtype)
            unit, _ = unit_and_root(kv_refs[j][0, h])
            term = part * unit
            k_all += jnp.sum(term, axis=0, keepdims=True)
            k_text += jnp.sum(jnp.where(text_mask(kv_block(k, j, place)), term, 0.0), axis=0, keepdims=True)
        for slot in range(NQ if last else 0):
            part = dq_ref[h, pl.ds(q_offset(slot, place), BR), :]
            if slot == 0:
                dq_own[h] = part
            else:
                messages[slot - 1][h] = part.astype(BF16)
            unit, _ = unit_and_root(q_refs[slot][0, h])
            term = part * unit
            q_all += jnp.sum(term, axis=0, keepdims=True)
            q_text += jnp.sum(jnp.where(text_mask(q_block(slot, place)), term, 0.0), axis=0, keepdims=True)
    gains = jnp.concatenate(
        [q_text, q_all - q_text, k_text, k_all - k_text, jnp.zeros((4, HD), F32)], axis=0
    )
    gains = gains if first else gain_in[...] + gains
    gain_ref[...] = gains


def pair_sum_kernel(own, r1, r2, r3, keep_ref, send_ref):
    def total(j, i):
        return own[j, i] + r1[j, i].astype(F32) + r2[j, i].astype(F32) + r3[j, i].astype(F32)

    for i in range(2):
        send_ref[i] = total(1, i).astype(BF16)
        keep_ref[i] = total(0, i)


def back(grad, raw, gain):
    unit, root = unit_and_root(raw)
    grad = grad * gain
    return (grad - unit * jnp.mean(grad * unit, axis=-1, keepdims=True)) * (1.0 / root)


def q_out_kernel(own, r1, r2, r3, raw, gain_ref, out):
    gain = gain_of(text_mask(q_block(0, here())), gain_ref)
    for h in range(NH):
        grad = own[h] + r1[h].astype(F32) + r2[h].astype(F32) + r3[h].astype(F32)
        out[h] = back(grad, raw[0, h], gain).astype(BF16)


def kv_out_kernel(keep, got, raw, gain_ref, k_out, v_out):
    gain = gain_of(text_mask(q_block(0, here())), gain_ref)
    for h in range(NH):
        k_out[h] = back(keep[0, h] + got[0, h].astype(F32), raw[0, h], gain).astype(BF16)
        v_out[h] = (keep[1, h] + got[1, h].astype(F32)).astype(BF16)


def kernel_call(kernel, outs, args, scratch=(), flops=0):
    whole = pl.BlockSpec(memory_space=pltpu.VMEM)
    size = sum(a.size * a.dtype.itemsize for a in args)
    return pl.pallas_call(
        kernel,
        out_shape=[jax.ShapeDtypeStruct(s, d) for s, d in outs],
        in_specs=[whole] * len(args),
        out_specs=[whole] * len(outs),
        scratch_shapes=list(scratch),
        compiler_params=pltpu.CompilerParams(vmem_limit_bytes=VMEM_LIMIT),
        cost_estimate=pl.CostEstimate(flops=flops, bytes_accessed=size, transcendentals=0),
    )(*args)


def fetch(a, axis, n, k):
    return lax.ppermute(a, axis, [((i + k) % n, i) for i in range(n)])


def swap(a, axis, n, k):
    return lax.ppermute(a, axis, [(i, i ^ k) for i in range(n)])


def give(a, axis, n, k):
    return lax.ppermute(a, axis, [(i, (i + k) % n) for i in range(n)])


def mirror(a):
    n = NZ * NQ
    return lax.ppermute(a, ("zk", "zq"), [(i, n - 1 - i) for i in range(n)])


def summed(a, axis, n, *others):
    terms = [a] + [swap(a, axis, n, k) for k in range(1, n)]
    terms = lax.optimization_barrier((*terms, *others))[:n]
    return (terms[0] + terms[1]) + (terms[2] + terms[3])


def after(a, *others):
    return lax.optimization_barrier((a, *others))[0]


def local(q_raw, k_raw, values, out_grad, q_gain, k_gain):
    def heads_first(a):
        return jnp.transpose(a, (1, 0, 2))

    kv = jnp.stack([heads_first(k_raw), heads_first(values)])
    qd = jnp.stack([heads_first(q_raw), heads_first(out_grad)])
    pair = mirror(kv)
    x1, x2, x3 = [fetch(kv, "x", NX, k) for k in range(1, NX)]
    q3 = swap(qd, "zq", NQ, 3)
    q2 = swap(after(qd, q3), "zq", NQ, 2)
    q1 = swap(after(qd, pair), "zq", NQ, 1)
    x1, x3, x2, pair = lax.optimization_barrier((x1, x3, x2, pair))
    p1, p2, p3 = [fetch(pair, "x", NX, k) for k in range(1, NX)]
    kvs = [kv, pair, x1, p1, x2, p2, x3, p3]
    qds = [qd, q1, q2, q3]
    tile = NH * QR * KR * HD * 2
    stat_shape, q_shape, k_shape = ((16, QR), F32), ((NH, QR, HD), BF16), ((NH, NX * BR, HD), BF16)
    stat, qn, do, kn_own, v_own = kernel_call(
        own_stat_kernel,
        [stat_shape, q_shape, q_shape, k_shape, k_shape],
        [*qds, kv, x1, x2, x3, q_gain, k_gain],
        flops=tile,
    )
    pairs = []
    for slots, blocks in (((0, 2), (pair, p2)), ((1, 3), (p1, p3))):
        stat, *kn_and_v = kernel_call(
            functools.partial(pair_stat_kernel, slots),
            [stat_shape, ((NH, KC, HD), BF16), ((NH, KC, HD), BF16)],
            [stat, qn, do, *blocks, k_gain],
            flops=tile // 2,
        )
        pairs.append(kn_and_v)
    stats = [stat] + [swap(stat, "zq", NQ, k) for k in (1, 2, 3)]
    part = (NH, BR, HD)
    kv_part = (NZ, 2, NH, BR, HD)
    whole_dq, gain_part = ((NH, QR, HD), F32), ((8, HD), F32)
    kv_got, carried = [], []
    for k in (2, 1, 3, 0):
        first, last = k == 2, k == 0
        outs = [(kv_part, F32 if last else BF16)]
        outs += [(part, F32)] + [(part, BF16)] * 3 if last else [whole_dq]
        args = [*stats, *kvs[NZ * k : NZ * k + NZ], *(qds if last else ()), qn, do, kn_own, v_own, *pairs[k % 2], *carried]
        got = kernel_call(
            functools.partial(grad_kernel, k, first, last),
            outs + [gain_part],
            args,
            scratch=[pltpu.VMEM((NH, QR, HD), F32)] if last else (),
            flops=6 * tile // NX,
        )
        if last:
            own, dq_own, *messages, gains = got
        else:
            kv_got.append(give(got[0], "x", NX, k))
            carried = got[1:]
    gains = summed(gains, "zq", NQ, kv_got[0])
    messages = [swap(m, "zq", NQ, k) for k, m in enumerate(messages, 1)]
    gains = gains + swap(gains, "core", 2, 1)
    gains = gains + mirror(gains)
    keep, send = kernel_call(
        pair_sum_kernel, [((2, NH, BR, HD), F32), ((2, NH, BR, HD), BF16)], [own, *kv_got]
    )
    got = mirror(send)
    gains = summed(gains, "y", 4, *messages)
    (q_out,) = kernel_call(q_out_kernel, [(part, BF16)], [dq_own, *messages, qd, q_gain])
    gains = summed(after(gains, send), "x", NX, got)
    k_out, v_out = kernel_call(
        kv_out_kernel, [(part, BF16)] * 2, [keep, got, kv, k_gain]
    )

    return (
        heads_first(q_out), heads_first(k_out), heads_first(v_out), gains[0:2], gains[2:4],
    )


def solution(mesh):
    torus = Mesh(mesh.devices.reshape(2, 4, 4, 4, 2), ("zk", "zq", "x", "y", "core"))
    placed = P(ALL_ROWS, ("y", "core"), None)
    return jax.shard_map(
        local,
        mesh=torus,
        in_specs=(placed,) * 4 + (P(), P()),
        out_specs=(placed,) * 3 + (P(), P()),
        check_vma=False,
    )
```

```python
import functools
import math

import jax
import jax.numpy as jnp
from jax import lax
from jax.experimental import pallas as pl
from jax.experimental.pallas import tpu as pltpu
from jax.sharding import Mesh
from jax.sharding import PartitionSpec as P

TXT = 512
EPS = 1e-06
NH, HD, BR = 3, 128, 144
NQ, NX, NZ = 4, 4, 2
QR = NQ * BR
KC = NZ * BR
KR = NX * KC
FACTOR = 1.0 / math.sqrt(HD)
SCALE2 = FACTOR * math.log2(math.e)
F32, BF16 = jnp.float32, jnp.bfloat16
VMEM_LIMIT = 24 * 1024 * 1024
ALL_ROWS = ("zk", "zq", "x")


def nt_dot(a, b):
    return lax.dot_general(a, b, (((1,), (1,)), ((), ())), preferred_element_type=F32)


def nn_dot(a, b):
    return lax.dot_general(a, b, (((1,), (0,)), ((), ())), preferred_element_type=F32)


def tn_dot(a, b):
    return lax.dot_general(a, b, (((0,), (0,)), ((), ())), preferred_element_type=F32)


def text_mask(block):
    row = block * BR + lax.broadcasted_iota(jnp.int32, (BR, 1), 0)
    return row < TXT


def unit_and_root(raw):
    wide = raw.astype(F32)
    root = jnp.sqrt(jnp.mean(wide * wide, axis=-1, keepdims=True) + EPS)
    return wide * (1.0 / root), root


def gain_of(mask, gain_ref):
    return jnp.where(mask, gain_ref[0:1, :], gain_ref[1:2, :])


def here():
    return lax.axis_index("zq"), lax.axis_index("zk"), lax.axis_index("x")


def q_block(slot, place):
    zq, zk, x = place
    return (NQ * zk + (zq ^ slot)) * NX + x


def kv_block(xslot, j, place):
    zq, zk, x = place
    z = NQ * zk + zq
    return ((NQ * NZ - 1 - z) if j else z) * NX + lax.rem(x + xslot, NX)


def q_offset(slot, place):
    return pl.multiple_of((place[0] ^ slot) * BR, 16)


def place_keys(refs, slots, j, gk_ref, kn_ref, v_ref):
    for at, (k, ref) in enumerate(zip(slots, refs)):
        gain = gain_of(text_mask(kv_block(k, j, here())), gk_ref)
        rows = pl.ds(at * BR, BR)
        for h in range(NH):
            unit, _ = unit_and_root(ref[0, h])
            kn_ref[h, rows, :] = (unit * gain).astype(BF16)
            v_ref[h, rows, :] = ref[1, h]


def fold_stats(qn_ref, do_ref, kn_ref, v_ref, before_ref, stat_ref):
    for h in range(NH):
        top = total = dot = None
        if before_ref is not None:
            top, total, dot = [before_ref[3 * h + i : 3 * h + i + 1, :] for i in range(3)]
        for at in range(0, kn_ref.shape[1], KC):
            rows = pl.ds(at, KC)
            s = nt_dot(kn_ref[h, rows, :], qn_ref[h]) * SCALE2
            g = nt_dot(v_ref[h, rows, :], do_ref[h])
            peak = jnp.max(s, axis=0, keepdims=True)
            new = peak if top is None else jnp.maximum(top, peak)
            w = jnp.exp2(s - new)
            part = jnp.sum(w, axis=0, keepdims=True)
            dpart = jnp.sum(w * g, axis=0, keepdims=True)
            if top is None:
                total, dot = part, dpart
            else:
                keep = jnp.exp2(top - new)
                total, dot = total * keep + part, dot * keep + dpart
            top = new
        stat_ref[3 * h : 3 * h + 1, :] = top
        stat_ref[3 * h + 1 : 3 * h + 2, :] = total
        stat_ref[3 * h + 2 : 3 * h + 3, :] = dot


def own_stat_kernel(q0, q1, q2, q3, kv0, kv1, kv2, kv3, gq_ref, gk_ref, stat_ref, qn_ref, do_ref, kn_ref, v_ref):
    place = here()
    for slot, ref in enumerate((q0, q1, q2, q3)):
        gain = gain_of(text_mask(q_block(slot, place)), gq_ref)
        rows = pl.ds(q_offset(slot, place), BR)
        for h in range(NH):
            unit, _ = unit_and_root(ref[0, h])
            qn_ref[h, rows, :] = (unit * gain).astype(BF16)
            do_ref[h, rows, :] = ref[1, h]
    place_keys((kv0, kv1, kv2, kv3), range(NX), 0, gk_ref, kn_ref, v_ref)
    stat_ref[...] = jnp.zeros_like(stat_ref)
    fold_stats(qn_ref, do_ref, kn_ref, v_ref, None, stat_ref)


def pair_stat_kernel(slots, before_ref, qn_ref, do_ref, kv_a, kv_b, gk_ref, stat_ref, kn_ref, v_ref):
    place_keys((kv_a, kv_b), slots, 1, gk_ref, kn_ref, v_ref)
    stat_ref[...] = jnp.zeros_like(stat_ref)
    fold_stats(qn_ref, do_ref, kn_ref, v_ref, before_ref, stat_ref)


def grad_kernel(k, first, last, *refs):
    s_refs, refs = refs[:NQ], refs[NQ:]
    kv_refs, refs = refs[:NZ], refs[NZ:]
    q_refs, refs = (refs[:NQ], refs[NQ:]) if last else ((), refs)
    qn_ref, do_ref, kn_own, v_own, kn_pair, v_pair, *refs = refs
    if first:
        kv_out, dq_ref, gain_ref = refs
    elif last:
        dq_in, gain_in, kv_out, dq_own, *messages, gain_ref, dq_ref = refs
    else:
        dq_in, gain_in, kv_out, dq_ref, gain_ref = refs
    place = here()
    k_text = jnp.zeros((1, HD), F32)
    k_all = jnp.zeros((1, HD), F32)
    q_text = jnp.zeros((1, HD), F32)
    q_all = jnp.zeros((1, HD), F32)
    rows, pair_rows = pl.ds(k * BR, BR), pl.ds(k // 2 * BR, BR)
    for h in range(NH):
        tops = [r[3 * h : 3 * h + 1, :] for r in s_refs]
        top = functools.reduce(jnp.maximum, tops)
        shares = [jnp.exp2(t - top) for t in tops]
        total = sum(r[3 * h + 1 : 3 * h + 2, :] * e for r, e in zip(s_refs, shares))
        row_dot = sum(r[3 * h + 2 : 3 * h + 3, :] * e for r, e in zip(s_refs, shares)) / total
        log_total = top + jnp.log2(total)
        kn = jnp.concatenate([kn_own[h, rows, :], kn_pair[h, pair_rows, :]], axis=0)
        v = jnp.concatenate([v_own[h, rows, :], v_pair[h, pair_rows, :]], axis=0)
        s = nt_dot(kn, qn_ref[h]) * SCALE2
        g = nt_dot(v, do_ref[h])
        p = jnp.exp2(s - log_total)
        low = p.astype(BF16)
        mixed = (p * g).astype(BF16)
        gs = (p * (g - row_dot)).astype(BF16)
        dv = nn_dot(low, do_ref[h])
        dk = nn_dot(gs, qn_ref[h]) * FACTOR
        dq = (tn_dot(kn, mixed) - row_dot * tn_dot(kn, low)) * FACTOR
        dq = jnp.transpose(dq, (1, 0))
        dq_ref[h] = dq if first else dq_in[h] + dq
        for j in range(NZ):
            part = dk[j * BR : (j + 1) * BR]
            kv_out[j, 0, h] = part.astype(kv_out.dtype)
            kv_out[j, 1, h] = dv[j * BR : (j + 1) * BR].astype(kv_out.dtype)
            unit, _ = unit_and_root(kv_refs[j][0, h])
            term = part * unit
            k_all += jnp.sum(term, axis=0, keepdims=True)
            k_text += jnp.sum(jnp.where(text_mask(kv_block(k, j, place)), term, 0.0), axis=0, keepdims=True)
        for slot in range(NQ if last else 0):
            part = dq_ref[h, pl.ds(q_offset(slot, place), BR), :]
            if slot == 0:
                dq_own[h] = part
            else:
                messages[slot - 1][h] = part.astype(BF16)
            unit, _ = unit_and_root(q_refs[slot][0, h])
            term = part * unit
            q_all += jnp.sum(term, axis=0, keepdims=True)
            q_text += jnp.sum(jnp.where(text_mask(q_block(slot, place)), term, 0.0), axis=0, keepdims=True)
    gains = jnp.concatenate(
        [q_text, q_all - q_text, k_text, k_all - k_text, jnp.zeros((4, HD), F32)], axis=0
    )
    gains = gains if first else gain_in[...] + gains
    gain_ref[...] = gains


def pair_sum_kernel(own, r1, r2, r3, keep_ref, send_ref):
    def total(j, i):
        return own[j, i] + r1[j, i].astype(F32) + r2[j, i].astype(F32) + r3[j, i].astype(F32)

    for i in range(2):
        send_ref[i] = total(1, i).astype(BF16)
        keep_ref[i] = total(0, i)


def back(grad, raw, gain):
    unit, root = unit_and_root(raw)
    grad = grad * gain
    return (grad - unit * jnp.mean(grad * unit, axis=-1, keepdims=True)) * (1.0 / root)


def q_out_kernel(own, r1, r2, r3, raw, gain_ref, out):
    gain = gain_of(text_mask(q_block(0, here())), gain_ref)
    for h in range(NH):
        grad = own[h] + r1[h].astype(F32) + r2[h].astype(F32) + r3[h].astype(F32)
        out[h] = back(grad, raw[0, h], gain).astype(BF16)


def kv_out_kernel(keep, got, raw, gain_ref, k_out, v_out):
    gain = gain_of(text_mask(q_block(0, here())), gain_ref)
    for h in range(NH):
        k_out[h] = back(keep[0, h] + got[0, h].astype(F32), raw[0, h], gain).astype(BF16)
        v_out[h] = (keep[1, h] + got[1, h].astype(F32)).astype(BF16)


def kernel_call(kernel, outs, args, scratch=(), flops=0):
    whole = pl.BlockSpec(memory_space=pltpu.VMEM)
    size = sum(a.size * a.dtype.itemsize for a in args)
    return pl.pallas_call(
        kernel,
        out_shape=[jax.ShapeDtypeStruct(s, d) for s, d in outs],
        in_specs=[whole] * len(args),
        out_specs=[whole] * len(outs),
        scratch_shapes=list(scratch),
        compiler_params=pltpu.CompilerParams(vmem_limit_bytes=VMEM_LIMIT),
        cost_estimate=pl.CostEstimate(flops=flops, bytes_accessed=size, transcendentals=0),
    )(*args)


def fetch(a, axis, n, k):
    return lax.ppermute(a, axis, [((i + k) % n, i) for i in range(n)])


def swap(a, axis, n, k):
    return lax.ppermute(a, axis, [(i, i ^ k) for i in range(n)])


def give(a, axis, n, k):
    return lax.ppermute(a, axis, [(i, (i + k) % n) for i in range(n)])


def mirror(a):
    n = NZ * NQ
    return lax.ppermute(a, ("zk", "zq"), [(i, n - 1 - i) for i in range(n)])


def summed(a, axis, n, *others):
    terms = [a] + [swap(a, axis, n, k) for k in range(1, n)]
    terms = lax.optimization_barrier((*terms, *others))[:n]
    return (terms[0] + terms[1]) + (terms[2] + terms[3])


def after(a, *others):
    return lax.optimization_barrier((a, *others))[0]


def local(q_raw, k_raw, values, out_grad, q_gain, k_gain):
    def heads_first(a):
        return jnp.transpose(a, (1, 0, 2))

    kv = jnp.stack([heads_first(k_raw), heads_first(values)])
    qd = jnp.stack([heads_first(q_raw), heads_first(out_grad)])
    pair = mirror(kv)
    x1, x2, x3 = [fetch(kv, "x", NX, k) for k in range(1, NX)]
    q3 = swap(qd, "zq", NQ, 3)
    q2 = swap(after(qd, q3), "zq", NQ, 2)
    q1 = swap(after(qd, pair), "zq", NQ, 1)
    x1, x3, x2, pair = lax.optimization_barrier((x1, x3, x2, pair))
    p1, p2, p3 = [fetch(pair, "x", NX, k) for k in range(1, NX)]
    kvs = [kv, pair, x1, p1, x2, p2, x3, p3]
    qds = [qd, q1, q2, q3]
    tile = NH * QR * KR * HD * 2
    stat_shape, q_shape, k_shape = ((16, QR), F32), ((NH, QR, HD), BF16), ((NH, NX * BR, HD), BF16)
    stat, qn, do, kn_own, v_own = kernel_call(
        own_stat_kernel,
        [stat_shape, q_shape, q_shape, k_shape, k_shape],
        [*qds, kv, x1, x2, x3, q_gain, k_gain],
        flops=tile,
    )
    pairs = []
    for slots, blocks in (((0, 2), (pair, p2)), ((1, 3), (p1, p3))):
        stat, *kn_and_v = kernel_call(
            functools.partial(pair_stat_kernel, slots),
            [stat_shape, ((NH, KC, HD), BF16), ((NH, KC, HD), BF16)],
            [stat, qn, do, *blocks, k_gain],
            flops=tile // 2,
        )
        pairs.append(kn_and_v)
    stats = [stat] + [swap(stat, "zq", NQ, k) for k in (1, 2, 3)]
    part = (NH, BR, HD)
    kv_part = (NZ, 2, NH, BR, HD)
    whole_dq, gain_part = ((NH, QR, HD), F32), ((8, HD), F32)
    kv_got, carried = [], []
    for k in (2, 1, 3, 0):
        first, last = k == 2, k == 0
        outs = [(kv_part, F32 if last else BF16)]
        outs += [(part, F32)] + [(part, BF16)] * 3 if last else [whole_dq]
        args = [*stats, *kvs[NZ * k : NZ * k + NZ], *(qds if last else ()), qn, do, kn_own, v_own, *pairs[k % 2], *carried]
        got = kernel_call(
            functools.partial(grad_kernel, k, first, last),
            outs + [gain_part],
            args,
            scratch=[pltpu.VMEM((NH, QR, HD), F32)] if last else (),
            flops=6 * tile // NX,
        )
        if last:
            own, dq_own, *messages, gains = got
        else:
            kv_got.append(give(got[0], "x", NX, k))
            carried = got[1:]
    gains = gains + swap(gains, "zq", NQ, 1)
    gains, other, *_ = lax.optimization_barrier((gains, swap(gains, "zq", NQ, 2), kv_got[0]))
    gains = gains + other
    messages = [swap(m, "zq", NQ, k) for k, m in enumerate(messages, 1)]
    gains = gains + swap(gains, "core", 2, 1)
    gains = gains + mirror(gains)
    keep, send = kernel_call(
        pair_sum_kernel, [((2, NH, BR, HD), F32), ((2, NH, BR, HD), BF16)], [own, *kv_got]
    )
    got = mirror(send)
    gains = summed(gains, "y", 4, *messages)
    (q_out,) = kernel_call(q_out_kernel, [(part, BF16)], [dq_own, *messages, qd, q_gain])
    k_out, v_out = kernel_call(kv_out_kernel, [(part, BF16)] * 2, [keep, got, kv, k_gain])
    gains = after(gains, send)
    terms = [gains] + [swap(gains, "x", NX, k) for k in range(1, NX)]
    terms = lax.optimization_barrier((*terms, k_out))[:NX]

    def gain_grad(rows):
        a, b, c, d = [t[rows] for t in terms]
        return (a + b) + (c + d)


    return (
        heads_first(q_out), heads_first(k_out), heads_first(v_out), gain_grad(slice(0, 2)), gain_grad(slice(2, 4)),
    )


def solution(mesh):
    torus = Mesh(mesh.devices.reshape(2, 4, 4, 4, 2), ("zk", "zq", "x", "y", "core"))
    placed = P(ALL_ROWS, ("y", "core"), None)
    return jax.shard_map(
        local,
        mesh=torus,
        in_specs=(placed,) * 4 + (P(), P()),
        out_specs=(placed,) * 3 + (P(), P()),
        check_vma=False,
    )
```
